768 devices in a mesh: mem: 96 (over z, x, core), grp: 8 (over y).
Axes of the slice: x: 4, y: 8, z: 12, core: 2. Of those that a mesh axis runs over, the one named last changes fastest.
Arguments:
- state: float32 [1024, 768, 128], P('grp', 'mem'), may hold values from -6 to 6
- obs_ens: float32 [1024, 768, 128], P('grp', 'mem'), may hold values from -6 to 6
- obs_value: float32 [768, 128], P(('mem', 'grp')), may hold values from -8 to 8
- obs_precision: float32 [768, 128], P(('mem', 'grp')), may hold values from 0.5 to 4
- locality: int32 [768, 384], P(('mem', 'grp')), may hold values from 0 to 383, as said below
- obs_count: int32 [768], P(('mem', 'grp')), may hold values from 48 to 384, as said below
- land_mask: int32 [768, 128], P(('mem', 'grp')), may hold values 0 or 1
Outputs:
- analysis: float32 [1024, 768, 128], P(None, ('mem', 'grp'))
The draws below stay inside these ranges and needn't reach their ends.
Inputs may be any that keep to these rules, and one draw needn't show every extreme that they name: `locality`: pool indices 0 to 127 name the previous patch's observations, 128 to 255 the patch's own, the rest the next patch's; every row lists each pool index once. `obs_count`: some patch has all 384 rows live.
All inputs are finite; a program needn't handle non-finite values. No bound on the sum of `land_mask` on one device may be relied on, other than what follows from the above.
Results may differ from the reference program's by a relative error of at most 0.0003.
Values sent between devices are 32-bit elements; how exact they have to be, the bound alone decides.
No kernel may reach another device: no remote copies, remote signals or barrier semaphores. Data moves between devices by JAX's collectives and lax.ppermute only.
A program may use at most 64 MiB of HBM per device.

```python
import math
import jax
import jax.numpy as jnp
from jax import lax

K = 1024
CELLS = 128
OWN = 128
LOCAL = 384
PATCHES = 768


def shuffle(subkey):
    return jax.random.permutation(subkey, LOCAL)


def draw_locality(key, part):
    key = jax.random.fold_in(key, 11)
    subkeys = jax.random.split(key, PATCHES)
    return jax.vmap(shuffle)(subkeys).astype(jnp.int32)


def draw_obs_count(key, part):
    key = jax.random.fold_in(key, 12)
    count_key, hot_key = jax.random.split(key)
    counts = jax.random.randint(count_key, (PATCHES,), LOCAL // 8, 2 * LOCAL, dtype=jnp.int32)
    counts = jnp.minimum(counts, LOCAL)
    hottest = jax.random.randint(hot_key, (), 0, PATCHES, dtype=jnp.int32)
    return jnp.where(jnp.arange(PATCHES, dtype=jnp.int32) == hottest, LOCAL, counts).astype(jnp.int32)


def plant(values, own_key, smallest, high):
    extent = values.shape
    spot = [jax.random.randint(jax.random.fold_in(own_key, axis), (), 0, extent[axis]) for axis in range(len(extent))]
    values = values.at[tuple(spot)].set(smallest)
    longest = extent.index(max(extent))
    spot[longest] = (spot[longest] + 1) % extent[longest]
    return values.at[tuple(spot)].set(high)


def levels(rng, extent, cuts, low, high):
    gain = 1.0
    for position, shards_of in cuts:
        steps = jax.random.uniform(jax.random.fold_in(jax.random.fold_in(rng, 6), position), (shards_of,), jnp.float32, low / len(cuts), high / len(cuts))
        gain = gain * jnp.repeat(jnp.exp(steps), extent[position] // shards_of).reshape((-1,) + (1,) * (len(extent) - 1 - position))
    return gain


def normal_values(key, dims, deviation, bound, cuts=(), kind=jnp.bfloat16):
    values = jax.random.normal(key, dims, jnp.float32) * deviation
    if len(cuts) > 0:
        values = levels(key, dims, cuts, -0.22, 0.18) * values
    return jnp.clip(values, min=-bound, max=bound).astype(kind)


def setup_inputs(seed: int = 0) -> dict:
    key_list = jax.random.split(jax.random.key(seed), 8)
    return {
        "state": normal_values(key_list[0], (K, PATCHES, CELLS), 1.0, 6.0, ((0, 8), (1, 96)), jnp.float32),
        "obs_ens": normal_values(key_list[1], (K, PATCHES, OWN), 1.0, 6.0, ((0, 8), (1, 96)), jnp.float32),
        "obs_value": normal_values(key_list[2], (PATCHES, OWN), 1.5, 8.0, ((0, 768),), jnp.float32),
        "obs_precision": jnp.clip(jnp.exp(math.log(4.0) - 2.0794415 * jax.random.uniform(key_list[3], (PATCHES, OWN), jnp.float32) ** levels(key_list[3], (PATCHES, OWN), ((0, 768),), -0.2, 0.2)), 0.5, 4.0),
        "locality": draw_locality(jax.random.fold_in(key_list[7], 71), 0),
        "obs_count": draw_obs_count(jax.random.fold_in(key_list[7], 71), 0),
        "land_mask": plant((jax.random.randint(key_list[6], (PATCHES, CELLS), 0, 4) < 3).astype(jnp.int32), jax.random.fold_in(key_list[6], 1), 0, 1),
    }


highest = lax.Precision.HIGHEST

def finish(background, centred, weights, depart, gram_matrix, land_row):
    members = background.shape[0]
    system = gram_matrix + (members - 1) * jnp.eye(members, dtype=jnp.float32)
    factor = jnp.linalg.cholesky(system)
    forcing = jnp.dot(centred, weights * depart, precision=highest)[:, None]
    halfway = jax.scipy.linalg.solve_triangular(factor, forcing, lower=True)
    mean_weights = jax.scipy.linalg.solve_triangular(factor, halfway, lower=True, trans=1)[:, 0]
    state_mean = lax.optimization_barrier(jnp.mean(background, axis=0))
    deviate = background - state_mean
    spread = math.sqrt(members - 1) * jax.scipy.linalg.solve_triangular(factor, deviate, lower=True)
    increment = jnp.dot(mean_weights, deviate, precision=highest)
    analysed = state_mean + increment + spread
    return jnp.where(land_row > 0, analysed, background)

def prepare(pooled, values, precise, picks, live_count):
    chosen = jnp.take(pooled, picks, axis=1)
    obs_mean = lax.optimization_barrier(jnp.mean(chosen, axis=0))
    centred = chosen - obs_mean
    live = jnp.arange(picks.shape[0], dtype=jnp.int32) < live_count
    weights = jnp.where(live, jnp.take(precise, picks), jnp.float32(0.0))
    depart = jnp.take(values, picks) - obs_mean
    return (centred, weights, depart)

def reference(state, obs_ens, obs_value, obs_precision, locality, obs_count, land_mask):
    total = state.shape[1]
    members = state.shape[0]

    def single(patch):
        trio = jnp.stack([(patch + total - 1) % total, patch, (patch + 1) % total]).astype(jnp.int32)
        pooled = jnp.take(obs_ens, trio, axis=1).reshape(members, -1)
        values = jnp.take(obs_value, trio, axis=0).reshape(-1)
        precise = jnp.take(obs_precision, trio, axis=0).reshape(-1)
        background = jnp.take(state, patch, axis=1)
        centred, weights, depart = prepare(pooled, values, precise, locality[patch], obs_count[patch])
        gram_matrix = lax.dot_general(centred * weights, centred, (((1,), (1,)), ((), ())), precision=highest)
        return finish(background, centred, weights, depart, gram_matrix, land_mask[patch])
    result = lax.map(single, jnp.arange(total, dtype=jnp.int32))
    return jnp.transpose(result, (1, 0, 2))
```

```python
import jax
import jax.numpy as jnp
from jax import lax
from jax.experimental import pallas as pl
from jax.experimental.pallas import tpu as pltpu
from jax.sharding import PartitionSpec as P

CHAINS = 8
SUB = 16
CUT = 5
BLOCK = 128


def lane(x, i):
    return jnp.broadcast_to(x[:, i:i + 1], x.shape)


def split(x):
    hi = x.astype(jnp.bfloat16)
    rest = x - hi.astype(jnp.float32)
    mid = rest.astype(jnp.bfloat16)
    lo = (rest - mid.astype(jnp.float32)).astype(jnp.bfloat16)
    return hi, mid, lo


def left(x, axis):
    hi, mid, lo = split(x)
    return jnp.concatenate([hi, hi, mid, hi, lo, mid], axis=axis)


def right(x, axis):
    hi, mid, lo = split(x)
    return jnp.concatenate([hi, mid, hi, lo, hi, mid], axis=axis)


def dot(a, b, ca, cb):
    return lax.dot_general(a, b, (((ca,), (cb,)), ((), ())), preferred_element_type=jnp.float32)


def mm_nn(a, b):
    return dot(left(a, 1), right(b, 0), 1, 0)


def mm_nt(a, b):
    return dot(left(a, 1), right(b, 1), 1, 1)


def mm_tn(a, b):
    return dot(left(a, 0), right(b, 0), 0, 0)


def sub_block(mat, inv, wrow, q):
    iota = lax.broadcasted_iota(jnp.int32, (CHAINS, BLOCK), 1)
    base = q * SUB
    panels = SUB // 8

    def block(rows, first):
        return {(a, b): lane(rows[a], first + b) for a in range(8) for b in range(a, 8)}

    groups = [
        [mat[pl.ds(base + 8 * r + a, CHAINS, stride=BLOCK), :] for a in range(8)]
        for r in range(panels)
    ]
    coef = block(groups[0], base)
    for p in range(panels):
        first = base + 8 * p
        inside = (iota >= first) & (iota < first + 8)
        rows = [jnp.where(inside, jnp.where(iota == first + a, 1.0, 0.0), groups[p][a]) for a in range(8)]
        for r in range(p + 1, panels):
            groups[r] = [jnp.where(inside, 0.0, x) for x in groups[r]]
        done = []
        ahead = None
        for t in range(8):
            scale = lax.rsqrt(coef[t, t])
            w = rows[t] * scale
            done.append(w)
            inv[pl.ds(first + t, CHAINS, stride=BLOCK), :] = jnp.where(iota <= first + t, w, 0.0)
            wrow[pl.ds(8 * p + t, CHAINS, stride=SUB), :] = w
            m = {a: coef[t, a] * scale for a in range(t + 1, 8)}
            for a in range(t + 1, 8):
                for b in range(a, 8):
                    coef[a, b] = coef[a, b] - m[a] * m[b]
                rows[a] = rows[a] - m[a] * w
            if p + 1 < panels:
                if t == CUT:
                    ahead = block(groups[p + 1], first + 8)
                c = [lane(w, first + 8 + a) for a in range(8)]
                for a in range(8):
                    groups[p + 1][a] = groups[p + 1][a] - c[a] * w
                if t >= CUT:
                    for a in range(8):
                        for b in range(a, 8):
                            ahead[a, b] = ahead[a, b] - c[a] * c[b]
        if p + 1 < panels:
            coef = ahead
            for r in range(p + 2, panels):
                for a in range(8):
                    x = groups[r][a]
                    for t in range(8):
                        x = x - lane(done[t], base + 8 * r + a) * done[t]
                    groups[r][a] = x


def join(mat, wrow, q):
    base = q * SUB
    lanes = lax.broadcasted_iota(jnp.int32, (SUB, BLOCK), 1)
    drop = (lanes > lax.broadcasted_iota(jnp.int32, (SUB, BLOCK), 0) + base) & (lanes < base + SUB)
    below = BLOCK - base - SUB
    over = lax.broadcasted_iota(jnp.int32, (below, BLOCK), 1)
    clear = (over >= base) & (over < base + SUB)
    for c in range(CHAINS):
        w = wrow[c * SUB:(c + 1) * SUB, :]
        out = dot(left(w, 0), right(jnp.where(drop, 0.0, w), 0), 0, 0)
        at = pl.ds(c * BLOCK + base + SUB, below)
        mat[at, :] = jnp.where(clear, 0.0, mat[at, :]) - out[base + SUB:, :]


def inverse_factors(mat, inv, wrow):
    for q in range(BLOCK // SUB):
        sub_block(mat, inv, wrow, q)
        if (q + 1) * SUB < BLOCK:
            join(mat, wrow, q)


def at(k):
    return pl.ds(pl.multiple_of(k * BLOCK, BLOCK), BLOCK)


def analyse(members, own, before, after, state, value, precise, land, out, p00, p10, p11, p20, p21, p22,
            f, u, r, s, inv, wrow):
    blocks = members // BLOCK
    eye = (lax.broadcasted_iota(jnp.int32, (BLOCK, BLOCK), 0)
           == lax.broadcasted_iota(jnp.int32, (BLOCK, BLOCK), 1)).astype(jnp.float32)
    first_row = lax.broadcasted_iota(jnp.int32, (BLOCK, BLOCK), 0) == 0
    state_mean = jnp.mean(state[...], axis=0, keepdims=True)
    r[0:members, :] = state[...] - state_mean
    r[members:, :] = jnp.zeros((BLOCK, BLOCK), jnp.float32)
    for i, obs in enumerate((own, before, after)):
        scale = jnp.sqrt(precise[i:i + 1, :] * (1.0 / (members - 1)))
        mean = jnp.mean(obs[...], axis=0, keepdims=True)
        u[i, 0:members, :] = (obs[...] - mean) * scale
        u[i, members:, :] = jnp.where(first_row, (value[i:i + 1, :] - mean) * scale, 0.0)

    def gather(k, total):
        uk = [u[i, at(k), :] for i in range(3)]
        cols = right(jnp.concatenate([r[at(k), :]] + uk, axis=1), 0)
        rows = [left(x, 0) for x in uk]
        g0 = dot(rows[0], cols[:, :2 * BLOCK], 0, 0)
        g1 = dot(rows[1], cols[:, :3 * BLOCK], 0, 0)
        g2 = dot(rows[2], cols, 0, 0)
        new = [g0[:, :BLOCK], g1[:, :BLOCK], g2[:, :BLOCK], g0[:, BLOCK:], g1[:, BLOCK:2 * BLOCK], g1[:, 2 * BLOCK:],
               g2[:, BLOCK:2 * BLOCK], g2[:, 2 * BLOCK:3 * BLOCK], g2[:, 3 * BLOCK:]]
        dest = [f.at[0], f.at[1], f.at[2], p00, p10, p11, p20, p21, p22]
        prev = at(jnp.maximum(k - 1, 0))
        starts = [0.0, 0.0, 0.0, eye, 0.0, eye, 0.0, 0.0, eye]
        for ref, x, start in zip(dest, new, starts):
            ref[at(k), :] = x + jnp.where(k == 0, start, ref[prev, :])
        s[at(k + 1), :] = eye
        return total

    lax.fori_loop(0, blocks, gather, 0)
    s[at(0), :] = eye + sum(mm_nt(u[i, at(0), :], u[i, at(0), :]) for i in range(3))

    def stage(i, c):
        k = c + 1
        t = inv[at(c), :]
        lower = ([p10, p20], [p21], [])[i]
        parts = [ref[at(c), :] for ref in lower] + [u[i, at(k), :]]
        rows = mm_nt(jnp.concatenate(parts, axis=0), t)
        top = (2 - i) * BLOCK
        g = mm_nn(t, f[i, at(c), :])
        y = rows[top:, :]
        s[at(k), :] += mm_nt(y, y)
        change = mm_nn(rows, g)
        r[at(k), :] -= change[top:, :]
        for n in range(2 - i):
            f[i + 1 + n, at(c), :] -= change[n * BLOCK:(n + 1) * BLOCK, :]
        if top:
            upd = mm_nt(rows, rows[:top, :])
            u[i + 1, at(k), :] -= upd[top:, :BLOCK]
            if i == 0:
                p11[at(c), :] -= upd[:BLOCK, :BLOCK]
                p21[at(c), :] -= upd[BLOCK:top, :BLOCK]
                p22[at(c), :] -= upd[BLOCK:top, BLOCK:]
                u[2, at(k), :] -= upd[top:, BLOCK:]
            else:
                p22[at(c), :] -= upd[:BLOCK, :BLOCK]

    for i, diag in enumerate((p00, p11, p22)):
        inverse_factors(diag, inv, wrow)

        def body(c, carry, i=i):
            stage(i, c)
            return carry

        lax.fori_loop(0, CHAINS, body, 0)
    inverse_factors(s, inv, wrow)
    increment = -r[members:members + 1, :]
    wet = land[0:1, :] > 0

    def final(k, carry):
        spread = mm_nn(inv[at(k), :], r[at(k), :])
        out[at(k), :] = jnp.where(wet, state_mean + increment + spread, state[at(k), :])
        return carry

    lax.fori_loop(0, blocks, final, 0)


def compute(own, before, after, state, value, precise, land):
    members = own.shape[0]
    big = pltpu.VMEM((members, BLOCK), jnp.float32)
    return pl.pallas_call(
        lambda *refs: analyse(members, *refs),
        out_shape=jax.ShapeDtypeStruct((members, BLOCK), jnp.float32),
        scratch_shapes=[big] * 6 + [
            pltpu.VMEM((3, members, BLOCK), jnp.float32),
            pltpu.VMEM((3, members + BLOCK, BLOCK), jnp.float32),
            pltpu.VMEM((members + BLOCK, BLOCK), jnp.float32),
            pltpu.VMEM((members + BLOCK, BLOCK), jnp.float32),
            big,
            pltpu.VMEM((CHAINS * SUB, BLOCK), jnp.float32),
        ],
        compiler_params=pltpu.CompilerParams(vmem_limit_bytes=48 * 1024 * 1024),
    )(own, before, after, state, value, precise, land)


def ring(x, step):
    count = lax.axis_size(("mem", "grp"))
    return lax.ppermute(x, ("mem", "grp"), [(i, (i + step) % count) for i in range(count)])


def local(state, obs_ens, obs_value, obs_precision, locality, obs_count, land_mask):
    info = jnp.concatenate([obs_value, obs_precision], axis=0)
    info = jnp.stack([info, ring(info, 1), ring(info, -1)], axis=0)
    spots = jnp.roll(jnp.arange(3 * BLOCK, dtype=jnp.int32), -BLOCK).reshape(3, BLOCK)
    spots = jnp.stack([spots[0], spots[2], spots[1]], axis=0)
    rank = jnp.arange(locality.shape[1], dtype=jnp.int32)
    live = jnp.where(rank < obs_count[0], locality[0], -1)
    live = jnp.any(spots[:, None, :] == live[None, :, None], axis=1)
    value, precise = info[:, 0, :], jnp.where(live, info[:, 1, :], 0.0)
    whole_obs = lax.all_to_all(obs_ens, "grp", split_axis=1, concat_axis=0, tiled=True)[:, 0, :]
    whole_state = lax.all_to_all(state, "grp", split_axis=1, concat_axis=0, tiled=True)[:, 0, :]
    before, after = ring(whole_obs, 1), ring(whole_obs, -1)
    out = compute(whole_obs, before, after, whole_state, value, precise, land_mask)
    return out[:, None, :]


def solution(mesh):
    placed = (
        P("grp", "mem", None),
        P("grp", "mem", None),
        P(("mem", "grp"), None),
        P(("mem", "grp"), None),
        P(("mem", "grp"), None),
        P(("mem", "grp")),
        P(("mem", "grp"), None),
    )
    return jax.shard_map(
        local, mesh=mesh, in_specs=placed, out_specs=P(None, ("mem", "grp"), None), check_vma=False
    )
```

```python
import jax
import jax.numpy as jnp
from jax import lax
from jax.experimental import pallas as pl
from jax.experimental.pallas import tpu as pltpu
from jax.sharding import PartitionSpec as P

CHAINS = 8
SUB = 16
CUT = 4
BLOCK = 128


def lane(x, i):
    return jnp.broadcast_to(x[:, i:i + 1], x.shape)


def split(x):
    hi = x.astype(jnp.bfloat16)
    rest = x - hi.astype(jnp.float32)
    mid = rest.astype(jnp.bfloat16)
    lo = (rest - mid.astype(jnp.float32)).astype(jnp.bfloat16)
    return hi, mid, lo


def left(x, axis):
    hi, mid, lo = split(x)
    return jnp.concatenate([hi, hi, mid, hi, lo, mid], axis=axis)


def right(x, axis):
    hi, mid, lo = split(x)
    return jnp.concatenate([hi, mid, hi, lo, hi, mid], axis=axis)


def pair(x):
    hi, mid, lo = split(x)
    return (jnp.concatenate([hi, hi, mid, hi, lo, mid], axis=1), jnp.concatenate([hi, mid, hi, lo, hi, mid], axis=1))


def dot(a, b, ca, cb):
    return lax.dot_general(a, b, (((ca,), (cb,)), ((), ())), preferred_element_type=jnp.float32)


def sub_block(mat, inv, wrow, q):
    iota = lax.broadcasted_iota(jnp.int32, (CHAINS, BLOCK), 1)
    base = q * SUB
    panels = SUB // 8

    def block(rows, first):
        return {(a, b): lane(rows[a], first + b) for a in range(8) for b in range(a, 8)}

    groups = [
        [mat[pl.ds(base + 8 * r + a, CHAINS, stride=BLOCK), :] for a in range(8)]
        for r in range(panels)
    ]
    coef = block(groups[0], base)
    for p in range(panels):
        first = base + 8 * p
        inside = (iota >= first) & (iota < first + 8)
        rows = [jnp.where(inside, jnp.where(iota == first + a, 1.0, 0.0), groups[p][a]) for a in range(8)]
        for r in range(p + 1, panels):
            groups[r] = [jnp.where(inside, 0.0, x) for x in groups[r]]
        done = []
        ahead = None
        for t in range(8):
            scale = lax.rsqrt(coef[t, t])
            w = rows[t] * scale
            done.append(w)
            inv[pl.ds(first + t, CHAINS, stride=BLOCK), :] = jnp.where(iota <= first + t, w, 0.0)
            wrow[pl.ds(8 * p + t, CHAINS, stride=SUB), :] = w
            m = {a: coef[t, a] * scale for a in range(t + 1, 8)}
            for a in range(t + 1, 8):
                for b in range(a, 8):
                    coef[a, b] = coef[a, b] - m[a] * m[b]
                rows[a] = rows[a] - m[a] * w
            if p + 1 < panels:
                if t == CUT:
                    ahead = block(groups[p + 1], first + 8)
                c = [lane(w, first + 8 + a) for a in range(8)]
                for a in range(8):
                    groups[p + 1][a] = groups[p + 1][a] - c[a] * w
                if t >= CUT:
                    for a in range(8):
                        for b in range(a, 8):
                            ahead[a, b] = ahead[a, b] - c[a] * c[b]
        if p + 1 < panels:
            coef = ahead
            for r in range(p + 2, panels):
                for a in range(8):
                    x = groups[r][a]
                    for t in range(8):
                        x = x - lane(done[t], base + 8 * r + a) * done[t]
                    groups[r][a] = x


def join(mat, wrow, q):
    base = q * SUB
    lanes = lax.broadcasted_iota(jnp.int32, (SUB, BLOCK), 1)
    drop = (lanes > lax.broadcasted_iota(jnp.int32, (SUB, BLOCK), 0) + base) & (lanes < base + SUB)
    below = BLOCK - base - SUB
    over = lax.broadcasted_iota(jnp.int32, (below, BLOCK), 1)
    clear = (over >= base) & (over < base + SUB)
    for c in range(CHAINS):
        w = wrow[c * SUB:(c + 1) * SUB, :]
        out = dot(left(w, 0), right(jnp.where(drop, 0.0, w), 0), 0, 0)
        at = pl.ds(c * BLOCK + base + SUB, below)
        mat[at, :] = jnp.where(clear, 0.0, mat[at, :]) - out[base + SUB:, :]


def inverse_factors(mat, inv, wrow, beside=None):
    for q in range(BLOCK // SUB):
        if beside is not None:
            beside(q)
        sub_block(mat, inv, wrow, q)
        if (q + 1) * SUB < BLOCK:
            join(mat, wrow, q)


def at(k):
    return pl.ds(k * BLOCK, BLOCK)


def unit():
    return (lax.broadcasted_iota(jnp.int32, (BLOCK, BLOCK), 0)
            == lax.broadcasted_iota(jnp.int32, (BLOCK, BLOCK), 1)).astype(jnp.float32)


def scaled(joined, live, members, u):
    precise = jnp.where(live > 0, joined[members + 1:members + 2, :], 0.0)
    scale = jnp.sqrt(precise * (1.0 / (members - 1)))
    obs = joined[0:members, :]
    mean = jnp.mean(obs, axis=0, keepdims=True)
    u[...] = (obs - mean) * scale
    return (joined[members:members + 1, :] - mean) * scale


def begin(members, own, live, u0, row0, inv0, p00, wrow):
    row0[...] = jnp.broadcast_to(scaled(own, live[...], members, u0), row0.shape)
    total = unit()
    for k in range(members // BLOCK):
        uk = u0[at(k), :]
        total = total + dot(left(uk, 0), right(uk, 0), 0, 0)
        p00[at(k), :] = total
    inverse_factors(p00, inv0, wrow)


def factor(members, u0, row0, inv0, before, after, live,
           u1, u2, l10, l20, l21, inv1, inv2, y0, y1, y2, s, p11, p21, p22, wrow):
    eye = unit()
    first_row = lax.broadcasted_iota(jnp.int32, (BLOCK, BLOCK), 0) == 0
    row1 = scaled(before, live[0:1, :], members, u1)
    row2 = scaled(after, live[1:2, :], members, u2)

    def forcing(ref, row, c):
        if c + 1 < CHAINS:
            return ref[at(c + 1), :]
        return jnp.where(first_row, row, 0.0)

    carry = {}

    def add(name, x):
        carry[name] = carry[name] + x if name in carry else x
        return carry[name]

    for c in range(CHAINS):
        lhs = left(u1[at(c), :], 0)
        got = dot(lhs, right(jnp.concatenate([u0[at(c), :], u1[at(c), :]], axis=1), 0), 0, 0)
        p10 = add("p10", got[:, :BLOCK])
        gram = add("p11", got[:, BLOCK:])
        rows = dot(left(p10, 1), right(inv0[at(c), :], 1), 1, 1)
        l10[at(c), :] = rows
        lhs, rhs = pair(rows)
        p11[at(c), :] = eye + gram - dot(lhs, rhs, 1, 1)

    def beside_one(c):
        uk = [u0[at(c), :], u1[at(c), :], u2[at(c), :]]
        got = dot(left(uk[2], 0), right(jnp.concatenate(uk, axis=1), 0), 0, 0)
        p20 = add("p20", got[:, :BLOCK])
        g21 = add("p21", got[:, BLOCK:2 * BLOCK])
        g22 = add("p22", got[:, 2 * BLOCK:])
        rows = dot(left(jnp.concatenate([p20, forcing(u0, row0[0:1, :], c)], axis=0), 1),
                   right(inv0[at(c), :], 1), 1, 1)
        l20[at(c), :] = rows[:BLOCK]
        y0[at(c), :] = rows[BLOCK:]
        lhs, rhs = pair(rows)
        upd = dot(lhs, jnp.concatenate([right(l10[at(c), :], 1), rhs[:BLOCK]], axis=0), 1, 1)
        p21[at(c), :] = g21 - upd[:BLOCK, :BLOCK]
        p22[at(c), :] = eye + g22 - upd[:BLOCK, BLOCK:]
        y1[at(c), :] = forcing(u1, row1, c) - upd[BLOCK:, :BLOCK]
        y2[at(c), :] = forcing(u2, row2, c) - upd[BLOCK:, BLOCK:]
        if c + 1 < CHAINS:
            s[at(c + 1), :] = eye + dot(lhs[BLOCK:], rhs[BLOCK:], 1, 1)

    inverse_factors(p11, inv1, wrow, beside_one)
    for c in range(CHAINS):
        rows = dot(left(p21[at(c), :], 1), right(inv1[at(c), :], 1), 1, 1)
        l21[at(c), :] = rows
        lhs, rhs = pair(rows)
        p22[at(c), :] -= dot(lhs, rhs, 1, 1)

    def beside_two(c):
        if c == 0:
            lhs, rhs = pair(jnp.concatenate([u0[at(0), :], u1[at(0), :], u2[at(0), :]], axis=1))
            s[at(0), :] = eye + dot(lhs, rhs, 1, 1)
        rows = dot(left(y1[at(c), :], 1), right(inv1[at(c), :], 1), 1, 1)
        y1[at(c), :] = rows
        lhs, rhs = pair(rows)
        upd = dot(lhs, jnp.concatenate([right(l21[at(c), :], 1), rhs], axis=0), 1, 1)
        y2[at(c), :] -= upd[:, :BLOCK]
        if c + 1 < CHAINS:
            s[at(c + 1), :] += upd[:, BLOCK:]

    inverse_factors(p22, inv2, wrow, beside_two)
    for c in range(CHAINS):
        rows = dot(left(y2[at(c), :], 1), right(inv2[at(c), :], 1), 1, 1)
        y2[at(c), :] = rows
        if c + 1 < CHAINS:
            lhs, rhs = pair(rows)
            s[at(c + 1), :] += dot(lhs, rhs, 1, 1)


def apply(members, state, land, s_in, u0, u1, u2, inv0, inv1, inv2, l10, l20, l21, y0, y1, y2, out, s, r, inv, wrow):
    state_mean = jnp.mean(state[...], axis=0, keepdims=True)
    s[...] = s_in[...]
    carry = {}

    def beside(c):
        uk = [u0[at(c), :], u1[at(c), :], u2[at(c), :]]
        got = dot(left(state[at(c), :] - state_mean, 0), right(jnp.concatenate(uk, axis=1), 0), 0, 0)
        got = [got[:, i * BLOCK:(i + 1) * BLOCK] for i in range(3)]
        got = [x + y for x, y in zip(got, carry["f"])] if "f" in carry else got
        carry["f"] = got
        g = dot(left(got[0], 1), right(inv0[at(c), :], 1), 1, 1)
        upd = dot(left(g, 1), right(jnp.concatenate([l10[at(c), :], l20[at(c), :], y0[at(c), :]], axis=0), 1), 1, 1)
        g = dot(left(got[1] - upd[:, :BLOCK], 1), right(inv1[at(c), :], 1), 1, 1)
        more = dot(left(g, 1), right(jnp.concatenate([l21[at(c), :], y1[at(c), :]], axis=0), 1), 1, 1)
        last = got[2] - upd[:, BLOCK:2 * BLOCK] - more[:, :BLOCK]
        g = dot(left(last, 1), right(inv2[at(c), :], 1), 1, 1)
        r[at(c), :] = upd[:, 2 * BLOCK:] + more[:, BLOCK:] + dot(left(g, 1), right(y2[at(c), :], 1), 1, 1)

    inverse_factors(s, inv, wrow, beside)
    increment = dot(left(unit()[:8], 1), right(r[at(CHAINS - 1), :], 1), 1, 1)[0:1, :]
    shift = state_mean + increment
    wet = land[0:1, :] > 0
    for k in range(members // BLOCK):
        back = state[at(k), :]
        t = left(inv[at(k), :], 1)
        spread = dot(t, right(back - state_mean, 0), 1, 0)
        if k > 0:
            spread = spread - dot(t, right(r[at(k - 1), :], 1), 1, 1)
        out[at(k), :] = jnp.where(wet, shift + spread, back)


def call(kernel, members, outs, scratch, flops, *args):
    def shape(rows):
        return jax.ShapeDtypeStruct((rows, BLOCK), jnp.float32)

    return pl.pallas_call(
        lambda *refs: kernel(members, *refs),
        out_shape=tuple(shape(rows) for rows in outs),
        scratch_shapes=[pltpu.VMEM((members, BLOCK), jnp.float32)] * scratch
        + [pltpu.VMEM((CHAINS * SUB, BLOCK), jnp.float32)],
        compiler_params=pltpu.CompilerParams(vmem_limit_bytes=32 * 1024 * 1024),
        cost_estimate=pl.CostEstimate(flops=flops, bytes_accessed=2_000_000, transcendentals=0),
    )(*args)


def start(own, live):
    n = own.shape[0] - 8
    return call(begin, n, (n, 8, n), 1, 4_000_000_000, own, live[0:1])


def middle(u0, row0, inv0, before, after, live):
    n = u0.shape[0]
    return call(factor, n, (n,) * 11, 3, 10_000_000_000, u0, row0, inv0, before, after, live[1:3])


def finish(state, land, u0, inv0, mid):
    n = u0.shape[0]
    u1, u2, l10, l20, l21, inv1, inv2, y0, y1, y2, s = mid
    return call(apply, n, (n,), 3, 8_000_000_000, state, land, s, u0, u1, u2, inv0, inv1, inv2,
                l10, l20, l21, y0, y1, y2)[0]


def compute(own, before, after, state, value, precise, land):
    info = jnp.stack([value, precise], axis=1)
    own, before, after = (jnp.concatenate([x, info[i], jnp.zeros((6, BLOCK), jnp.float32)]) for i, x in enumerate((own, before, after)))
    live = jnp.ones((3, BLOCK), jnp.int32)
    u0, row0, inv0 = start(own, live)
    return finish(state, land, u0, inv0, middle(u0, row0, inv0, before, after, live))


def ring(x, step):
    count = lax.axis_size(("mem", "grp"))
    return lax.ppermute(x, ("mem", "grp"), [(i, (i + step) % count) for i in range(count)])


def local(state, obs_ens, obs_value, obs_precision, locality, obs_count, land_mask):
    spots = jnp.arange(3 * BLOCK, dtype=jnp.int32).reshape(3, BLOCK)
    spots = jnp.stack([spots[1], spots[0], spots[2]], axis=0)
    rank = jnp.arange(locality.shape[1], dtype=jnp.int32)
    live = jnp.where(rank < obs_count[0], locality[0], -1)
    live = jnp.any(spots[:, None, :] == live[None, :, None], axis=1).astype(jnp.int32)
    whole_obs = lax.all_to_all(obs_ens, "grp", split_axis=1, concat_axis=0, tiled=True)[:, 0, :]
    own = jnp.concatenate([whole_obs, obs_value, obs_precision, jnp.zeros((6, BLOCK), jnp.float32)], axis=0)
    before, after = ring(own, 1), ring(own, -1)
    u0, row0, inv0 = start(own, live)
    state, inv0 = lax.optimization_barrier((state, inv0))
    whole_state = lax.all_to_all(state, "grp", split_axis=1, concat_axis=0, tiled=True)[:, 0, :]
    mid = middle(u0, row0, inv0, before, after, live)
    out = finish(whole_state, land_mask, u0, inv0, mid)
    return out[:, None, :]


def solution(mesh):
    placed = (
        P("grp", "mem", None),
        P("grp", "mem", None),
        P(("mem", "grp"), None),
        P(("mem", "grp"), None),
        P(("mem", "grp"), None),
        P(("mem", "grp")),
        P(("mem", "grp"), None),
    )
    return jax.shard_map(
        local, mesh=mesh, in_specs=placed, out_specs=P(None, ("mem", "grp"), None), check_vma=False
    )
```

```python
import jax
import jax.numpy as jnp
from jax import lax
from jax.experimental import pallas as pl
from jax.experimental.pallas import tpu as pltpu
from jax.sharding import PartitionSpec as P

CHAINS = 8
SUB = 16
CUT = 4
BLOCK = 128


def lane(x, i):
    return jnp.broadcast_to(x[:, i:i + 1], x.shape)


def split(x):
    hi = x.astype(jnp.bfloat16)
    rest = x - hi.astype(jnp.float32)
    mid = rest.astype(jnp.bfloat16)
    lo = (rest - mid.astype(jnp.float32)).astype(jnp.bfloat16)
    return hi, mid, lo


def left(x, axis):
    hi, mid, lo = split(x)
    return jnp.concatenate([hi, hi, mid, hi, lo, mid], axis=axis)


def right(x, axis):
    hi, mid, lo = split(x)
    return jnp.concatenate([hi, mid, hi, lo, hi, mid], axis=axis)


def pair(x):
    hi, mid, lo = split(x)
    return (jnp.concatenate([hi, hi, mid, hi, lo, mid], axis=1), jnp.concatenate([hi, mid, hi, lo, hi, mid], axis=1))


def dot(a, b, ca, cb):
    return lax.dot_general(a, b, (((ca,), (cb,)), ((), ())), preferred_element_type=jnp.float32)


def sub_block(mat, inv, wrow, q):
    iota = lax.broadcasted_iota(jnp.int32, (CHAINS, BLOCK), 1)
    base = q * SUB
    panels = SUB // 8

    def block(rows, first):
        return {(a, b): lane(rows[a], first + b) for a in range(8) for b in range(a, 8)}

    groups = [
        [mat[pl.ds(base + 8 * r + a, CHAINS, stride=BLOCK), :] for a in range(8)]
        for r in range(panels)
    ]
    coef = block(groups[0], base)
    for p in range(panels):
        first = base + 8 * p
        inside = (iota >= first) & (iota < first + 8)
        rows = [jnp.where(inside, jnp.where(iota == first + a, 1.0, 0.0), groups[p][a]) for a in range(8)]
        for r in range(p + 1, panels):
            groups[r] = [jnp.where(inside, 0.0, x) for x in groups[r]]
        done = []
        ahead = None
        for t in range(8):
            scale = lax.rsqrt(coef[t, t])
            w = rows[t] * scale
            done.append(w)
            inv[pl.ds(first + t, CHAINS, stride=BLOCK), :] = jnp.where(iota <= first + t, w, 0.0)
            wrow[pl.ds(8 * p + t, CHAINS, stride=SUB), :] = w
            m = {a: coef[t, a] * scale for a in range(t + 1, 8)}
            for a in range(t + 1, 8):
                for b in range(a, 8):
                    coef[a, b] = coef[a, b] - m[a] * m[b]
                rows[a] = rows[a] - m[a] * w
            if p + 1 < panels:
                if t == CUT:
                    ahead = block(groups[p + 1], first + 8)
                c = [lane(w, first + 8 + a) for a in range(8)]
                for a in range(8):
                    groups[p + 1][a] = groups[p + 1][a] - c[a] * w
                if t >= CUT:
                    for a in range(8):
                        for b in range(a, 8):
                            ahead[a, b] = ahead[a, b] - c[a] * c[b]
        if p + 1 < panels:
            coef = ahead
            for r in range(p + 2, panels):
                for a in range(8):
                    x = groups[r][a]
                    for t in range(8):
                        x = x - lane(done[t], base + 8 * r + a) * done[t]
                    groups[r][a] = x


def join(mat, wrow, q):
    base = q * SUB
    lanes = lax.broadcasted_iota(jnp.int32, (SUB, BLOCK), 1)
    drop = (lanes > lax.broadcasted_iota(jnp.int32, (SUB, BLOCK), 0) + base) & (lanes < base + SUB)
    below = BLOCK - base - SUB
    over = lax.broadcasted_iota(jnp.int32, (below, BLOCK), 1)
    clear = (over >= base) & (over < base + SUB)
    for c in range(CHAINS):
        w = wrow[c * SUB:(c + 1) * SUB, :]
        out = dot(left(w, 0), right(jnp.where(drop, 0.0, w), 0), 0, 0)
        at = pl.ds(c * BLOCK + base + SUB, below)
        mat[at, :] = jnp.where(clear, 0.0, mat[at, :]) - out[base + SUB:, :]


def inverse_factors(mat, inv, wrow, stages=()):
    def beside(q):
        for step in range(max((len(group) for group in stages), default=0)):
            for d, group in enumerate(stages):
                if step < len(group) and 0 <= q - d < CHAINS:
                    group[step](q - d)

    count = BLOCK // SUB
    for q in range(count):
        beside(q)
        sub_block(mat, inv, wrow, q)
        if q + 1 < count:
            join(mat, wrow, q)
    for q in range(count, count + len(stages) - 1):
        beside(q)


def at(k):
    return pl.ds(k * BLOCK, BLOCK)


def unit():
    return (lax.broadcasted_iota(jnp.int32, (BLOCK, BLOCK), 0)
            == lax.broadcasted_iota(jnp.int32, (BLOCK, BLOCK), 1)).astype(jnp.float32)


def scaled(joined, live, members, u):
    precise = jnp.where(live > 0, joined[members + 1:members + 2, :], 0.0)
    scale = jnp.sqrt(precise * (1.0 / (members - 1)))
    obs = joined[0:members, :]
    mean = jnp.mean(obs, axis=0, keepdims=True)
    u[...] = (obs - mean) * scale
    return (joined[members:members + 1, :] - mean) * scale


def begin(members, own, live, u0, row0, inv0, p00, wrow):
    row0[...] = jnp.broadcast_to(scaled(own, live[...], members, u0), row0.shape)
    total = unit()
    for k in range(members // BLOCK):
        uk = u0[at(k), :]
        total = total + dot(left(uk, 0), right(uk, 0), 0, 0)
        p00[at(k), :] = total
    inverse_factors(p00, inv0, wrow)


def factor(members, u0, row0, inv0, before, after, live, *rest):
    outs, (u1, u2, l10, l20, l21, inv1, inv2, y0, y1, y2, s, p11, p21, p22, wrow, sems) = rest[:11], rest[11:]
    kept = (u1, u2, l10, l20, l21, inv1, inv2, y0, y1, y2, s)
    copies = [pltpu.make_async_copy(kept[i], outs[i], sems.at[i]) for i in range(11)]

    def send(*refs):
        for i in refs:
            copies[i].start()

    eye = unit()
    first_row = lax.broadcasted_iota(jnp.int32, (BLOCK, BLOCK), 0) == 0
    row1 = scaled(before, live[0:1, :], members, u1)
    row2 = scaled(after, live[1:2, :], members, u2)
    send(0, 1)

    def forcing(ref, row, c):
        if c + 1 < CHAINS:
            return ref[at(c + 1), :]
        return jnp.where(first_row, row, 0.0)

    for c in range(CHAINS):
        got = dot(left(u1[at(c), :], 0), right(jnp.concatenate([u0[at(c), :], u1[at(c), :]], axis=1), 0), 0, 0)
        l10[at(c), :] = got[:, :BLOCK] + (l10[at(c - 1), :] if c else 0.0)
        p11[at(c), :] = got[:, BLOCK:] + (p11[at(c - 1), :] if c else eye)
    for c in range(CHAINS):
        l10[at(c), :] = dot(left(l10[at(c), :], 1), right(inv0[at(c), :], 1), 1, 1)
    send(2)
    for c in range(CHAINS):
        lhs, rhs = pair(l10[at(c), :])
        p11[at(c), :] -= dot(lhs, rhs, 1, 1)

    def gram(c):
        uk = [u0[at(c), :], u1[at(c), :], u2[at(c), :]]
        got = dot(left(uk[2], 0), right(jnp.concatenate(uk, axis=1), 0), 0, 0)
        l20[at(c), :] = got[:, :BLOCK] + (l20[at(c - 1), :] if c else 0.0)
        p21[at(c), :] = got[:, BLOCK:2 * BLOCK] + (p21[at(c - 1), :] if c else 0.0)
        p22[at(c), :] = got[:, 2 * BLOCK:] + (p22[at(c - 1), :] if c else eye)

    def low(c):
        rows = dot(left(jnp.concatenate([l20[at(c), :], forcing(u0, row0[0:1, :], c)], axis=0), 1),
                   right(inv0[at(c), :], 1), 1, 1)
        l20[at(c), :] = rows[:BLOCK]
        y0[at(c), :] = rows[BLOCK:]

    def take(c):
        lhs, rhs = pair(jnp.concatenate([l20[at(c), :], y0[at(c), :]], axis=0))
        upd = dot(lhs, jnp.concatenate([right(l10[at(c), :], 1), rhs[:BLOCK]], axis=0), 1, 1)
        p21[at(c), :] -= upd[:BLOCK, :BLOCK]
        p22[at(c), :] -= upd[:BLOCK, BLOCK:]
        y1[at(c), :] = forcing(u1, row1, c) - upd[BLOCK:, :BLOCK]
        y2[at(c), :] = forcing(u2, row2, c) - upd[BLOCK:, BLOCK:]
        if c + 1 < CHAINS:
            s[at(c + 1), :] = eye + dot(lhs[BLOCK:], rhs[BLOCK:], 1, 1)

    inverse_factors(p11, inv1, wrow, ((gram,), (low,), (take,)))
    send(3, 5, 7)
    for c in range(CHAINS):
        l21[at(c), :] = dot(left(p21[at(c), :], 1), right(inv1[at(c), :], 1), 1, 1)
    send(4)
    for c in range(CHAINS):
        lhs, rhs = pair(l21[at(c), :])
        p22[at(c), :] -= dot(lhs, rhs, 1, 1)

    def low_two(c):
        y1[at(c), :] = dot(left(y1[at(c), :], 1), right(inv1[at(c), :], 1), 1, 1)

    def take_two(c):
        lhs, rhs = pair(y1[at(c), :])
        upd = dot(lhs, jnp.concatenate([right(l21[at(c), :], 1), rhs], axis=0), 1, 1)
        y2[at(c), :] -= upd[:, :BLOCK]
        if c + 1 < CHAINS:
            s[at(c + 1), :] += upd[:, BLOCK:]
        else:
            lhs, rhs = pair(jnp.concatenate([u0[at(0), :], u1[at(0), :], u2[at(0), :]], axis=1))
            s[at(0), :] = eye + dot(lhs, rhs, 1, 1)

    inverse_factors(p22, inv2, wrow, ((low_two,), (take_two,)))
    send(6, 8)
    for c in range(CHAINS):
        y2[at(c), :] = dot(left(y2[at(c), :], 1), right(inv2[at(c), :], 1), 1, 1)
    send(9)
    for c in range(CHAINS - 1):
        lhs, rhs = pair(y2[at(c), :])
        s[at(c + 1), :] += dot(lhs, rhs, 1, 1)
    send(10)
    for copy in copies:
        copy.wait()


def apply(members, state, land, *rest):
    ins, out, rest = rest[:13], rest[13], rest[14:]
    s, u0, u1, u2, inv0, l10, l20, y0, inv1, l21, y1, inv2, y2, f0, f1, f2, r, inv, wrow, sems = rest
    kept = (s, u0, u1, u2, inv0, l10, l20, y0, inv1, l21, y1, inv2, y2)
    copies = [pltpu.make_async_copy(ins[i], kept[i], sems.at[i]) for i in range(13)]
    for copy in copies:
        copy.start()
    state_mean = jnp.mean(state[...], axis=0, keepdims=True)
    for copy in copies:
        copy.wait()

    def gram(c):
        uk = [u0[at(c), :], u1[at(c), :], u2[at(c), :]]
        got = dot(left(state[at(c), :] - state_mean, 0), right(jnp.concatenate(uk, axis=1), 0), 0, 0)
        for i, ref in enumerate((f0, f1, f2)):
            x = got[:, i * BLOCK:(i + 1) * BLOCK]
            ref[at(c + 1), :] = x + (ref[at(c), :] if c else 0.0)

    def low_one(c):
        r[at(c), :] = dot(left(f0[at(c + 1), :], 1), right(inv0[at(c), :], 1), 1, 1)

    def take_one(c):
        cols = jnp.concatenate([l10[at(c), :], l20[at(c), :], y0[at(c), :]], axis=0)
        upd = dot(left(r[at(c), :], 1), right(cols, 1), 1, 1)
        f1[at(c + 1), :] -= upd[:, :BLOCK]
        f2[at(c + 1), :] -= upd[:, BLOCK:2 * BLOCK]
        r[at(c), :] = upd[:, 2 * BLOCK:]

    def low_two(c):
        f1[at(c + 1), :] = dot(left(f1[at(c + 1), :], 1), right(inv1[at(c), :], 1), 1, 1)

    def take_two(c):
        upd = dot(left(f1[at(c + 1), :], 1), right(jnp.concatenate([l21[at(c), :], y1[at(c), :]], axis=0), 1), 1, 1)
        f2[at(c + 1), :] -= upd[:, :BLOCK]
        r[at(c), :] += upd[:, BLOCK:]

    def low_three(c):
        f2[at(c + 1), :] = dot(left(f2[at(c + 1), :], 1), right(inv2[at(c), :], 1), 1, 1)

    def take_three(c):
        r[at(c), :] += dot(left(f2[at(c + 1), :], 1), right(y2[at(c), :], 1), 1, 1)

    inverse_factors(s, inv, wrow, ((gram,), (low_one, take_one), (low_two, take_two), (low_three, take_three)))
    increment = dot(left(unit()[:8], 1), right(r[at(CHAINS - 1), :], 1), 1, 1)[0:1, :]
    shift = state_mean + increment
    wet = land[0:1, :] > 0
    for k in range(members // BLOCK):
        back = state[at(k), :]
        t = left(inv[at(k), :], 1)
        spread = dot(t, right(back - state_mean, 0), 1, 0)
        if k > 0:
            spread = spread - dot(t, right(r[at(k - 1), :], 1), 1, 1)
        out[at(k), :] = jnp.where(wet, shift + spread, back)


def call(kernel, members, outs, scratch, flops, args, far_in=0, far_out=0):
    far, near = pl.BlockSpec(memory_space=pltpu.HBM), pl.BlockSpec(memory_space=pltpu.VMEM)
    sems = [pltpu.SemaphoreType.DMA((far_in + far_out,))] if far_in + far_out else []
    return pl.pallas_call(
        lambda *refs: kernel(members, *refs),
        out_shape=tuple(jax.ShapeDtypeStruct((rows, BLOCK), jnp.float32) for rows in outs),
        in_specs=[near] * (len(args) - far_in) + [far] * far_in,
        out_specs=tuple([far] * far_out + [near] * (len(outs) - far_out)),
        scratch_shapes=[pltpu.VMEM((rows, BLOCK), jnp.float32) for rows in scratch]
        + [pltpu.VMEM((CHAINS * SUB, BLOCK), jnp.float32)] + sems,
        compiler_params=pltpu.CompilerParams(vmem_limit_bytes=32 * 1024 * 1024),
        cost_estimate=pl.CostEstimate(flops=flops, bytes_accessed=2_000_000, transcendentals=0),
    )(*args)


def start(own, live):
    n = own.shape[0] - 8
    return call(begin, n, (n, 8, n), (n,), 4_000_000_000, (own, live[0:1]))


def middle(u0, row0, inv0, before, after, live):
    n = u0.shape[0]
    return call(factor, n, (n,) * 11, (n,) * 14, 10_000_000_000, (u0, row0, inv0, before, after, live[1:3]), 0, 11)


def finish(state, land, u0, inv0, mid):
    n = u0.shape[0]
    u1, u2, l10, l20, l21, inv1, inv2, y0, y1, y2, s = mid
    far = (s, u0, u1, u2, inv0, l10, l20, y0, inv1, l21, y1, inv2, y2)
    return call(apply, n, (n,), (n,) * 13 + (n + BLOCK,) * 3 + (n, n), 8_000_000_000, (state, land) + far, 13, 0)[0]


def compute(own, before, after, state, value, precise, land):
    info = jnp.stack([value, precise], axis=1)
    own, before, after = (jnp.concatenate([x, info[i], jnp.zeros((6, BLOCK), jnp.float32)]) for i, x in enumerate((own, before, after)))
    live = jnp.ones((3, BLOCK), jnp.int32)
    u0, row0, inv0 = start(own, live)
    return finish(state, land, u0, inv0, middle(u0, row0, inv0, before, after, live))


def ring(x, step):
    count = lax.axis_size(("mem", "grp"))
    return lax.ppermute(x, ("mem", "grp"), [(i, (i + step) % count) for i in range(count)])


def local(state, obs_ens, obs_value, obs_precision, locality, obs_count, land_mask):
    spots = jnp.arange(3 * BLOCK, dtype=jnp.int32).reshape(3, BLOCK)
    spots = jnp.stack([spots[1], spots[0], spots[2]], axis=0)
    rank = jnp.arange(locality.shape[1], dtype=jnp.int32)
    live = jnp.where(rank < obs_count[0], locality[0], -1)
    live = jnp.any(spots[:, None, :] == live[None, :, None], axis=1).astype(jnp.int32)
    whole_obs = lax.all_to_all(obs_ens, "grp", split_axis=1, concat_axis=0, tiled=True)[:, 0, :]
    own = jnp.concatenate([whole_obs, obs_value, obs_precision, jnp.zeros((6, BLOCK), jnp.float32)], axis=0)
    before, after = ring(own, 1), ring(own, -1)
    u0, row0, inv0 = start(own, live)
    state, inv0 = lax.optimization_barrier((state, inv0))
    whole_state = lax.all_to_all(state, "grp", split_axis=1, concat_axis=0, tiled=True)[:, 0, :]
    mid = middle(u0, row0, inv0, before, after, live)
    out = finish(whole_state, land_mask, u0, inv0, mid)
    return out[:, None, :]


def solution(mesh):
    placed = (
        P("grp", "mem", None),
        P("grp", "mem", None),
        P(("mem", "grp"), None),
        P(("mem", "grp"), None),
        P(("mem", "grp"), None),
        P(("mem", "grp")),
        P(("mem", "grp"), None),
    )
    return jax.shard_map(
        local, mesh=mesh, in_specs=placed, out_specs=P(None, ("mem", "grp"), None), check_vma=False
    )
```

```python
import jax
import jax.numpy as jnp
from jax import lax
from jax.experimental import pallas as pl
from jax.experimental.pallas import tpu as pltpu
from jax.sharding import PartitionSpec as P

CHAINS = 8
SUB = 16
CUT = 4
BLOCK = 128


def lane(x, i):
    return jnp.broadcast_to(x[:, i:i + 1], x.shape)


def split(x):
    hi = x.astype(jnp.bfloat16)
    rest = x - hi.astype(jnp.float32)
    mid = rest.astype(jnp.bfloat16)
    lo = (rest - mid.astype(jnp.float32)).astype(jnp.bfloat16)
    return hi, mid, lo


def left(x, axis):
    hi, mid, lo = split(x)
    return jnp.concatenate([hi, hi, mid, hi, lo, mid], axis=axis)


def right(x, axis):
    hi, mid, lo = split(x)
    return jnp.concatenate([hi, mid, hi, lo, hi, mid], axis=axis)


def pair(x):
    hi, mid, lo = split(x)
    return (jnp.concatenate([hi, hi, mid, hi, lo, mid], axis=1), jnp.concatenate([hi, mid, hi, lo, hi, mid], axis=1))


def dot(a, b, ca, cb):
    return lax.dot_general(a, b, (((ca,), (cb,)), ((), ())), preferred_element_type=jnp.float32)


def sub_block(mat, inv, wrow, q):
    iota = lax.broadcasted_iota(jnp.int32, (CHAINS, BLOCK), 1)
    base = q * SUB
    panels = SUB // 8

    def block(rows, first):
        return {(a, b): lane(rows[a], first + b) for a in range(8) for b in range(a, 8)}

    groups = [
        [mat[pl.ds(base + 8 * r + a, CHAINS, stride=BLOCK), :] for a in range(8)]
        for r in range(panels)
    ]
    coef = block(groups[0], base)
    for p in range(panels):
        first = base + 8 * p
        inside = (iota >= first) & (iota < first + 8)
        rows = [jnp.where(inside, jnp.where(iota == first + a, 1.0, 0.0), groups[p][a]) for a in range(8)]
        for r in range(p + 1, panels):
            groups[r] = [jnp.where(inside, 0.0, x) for x in groups[r]]
        done = []
        ahead = None
        for t in range(8):
            scale = lax.rsqrt(coef[t, t])
            w = rows[t] * scale
            done.append(w)
            inv[pl.ds(first + t, CHAINS, stride=BLOCK), :] = jnp.where(iota <= first + t, w, 0.0)
            wrow[pl.ds(8 * p + t, CHAINS, stride=SUB), :] = w
            m = {a: coef[t, a] * scale for a in range(t + 1, 8)}
            for a in range(t + 1, 8):
                for b in range(a, 8):
                    coef[a, b] = coef[a, b] - m[a] * m[b]
                rows[a] = rows[a] - m[a] * w
            if p + 1 < panels:
                if t == CUT:
                    ahead = block(groups[p + 1], first + 8)
                c = [lane(w, first + 8 + a) for a in range(8)]
                for a in range(8):
                    groups[p + 1][a] = groups[p + 1][a] - c[a] * w
                if t >= CUT:
                    for a in range(8):
                        for b in range(a, 8):
                            ahead[a, b] = ahead[a, b] - c[a] * c[b]
        if p + 1 < panels:
            coef = ahead
            for r in range(p + 2, panels):
                for a in range(8):
                    x = groups[r][a]
                    for t in range(8):
                        x = x - lane(done[t], base + 8 * r + a) * done[t]
                    groups[r][a] = x


def join(mat, wrow, q):
    base = q * SUB
    lanes = lax.broadcasted_iota(jnp.int32, (SUB, BLOCK), 1)
    drop = (lanes > lax.broadcasted_iota(jnp.int32, (SUB, BLOCK), 0) + base) & (lanes < base + SUB)
    below = BLOCK - base - SUB
    over = lax.broadcasted_iota(jnp.int32, (below, BLOCK), 1)
    clear = (over >= base) & (over < base + SUB)
    for c in range(CHAINS):
        w = wrow[c * SUB:(c + 1) * SUB, :]
        out = dot(left(w, 0), right(jnp.where(drop, 0.0, w), 0), 0, 0)
        at = pl.ds(c * BLOCK + base + SUB, below)
        mat[at, :] = jnp.where(clear, 0.0, mat[at, :]) - out[base + SUB:, :]


def inverse_factors(mat, inv, wrow, stages=()):
    def beside(q):
        for step in range(max((len(group) for group in stages), default=0)):
            for d, group in enumerate(stages):
                if step < len(group) and 0 <= q - d < CHAINS:
                    group[step](q - d)

    count = BLOCK // SUB
    for q in range(count):
        beside(q)
        sub_block(mat, inv, wrow, q)
        if q + 1 < count:
            join(mat, wrow, q)
    for q in range(count, count + len(stages) - 1):
        beside(q)


def at(k):
    return pl.ds(k * BLOCK, BLOCK)


def unit():
    return (lax.broadcasted_iota(jnp.int32, (BLOCK, BLOCK), 0)
            == lax.broadcasted_iota(jnp.int32, (BLOCK, BLOCK), 1)).astype(jnp.float32)


def scaled(joined, live, members, u):
    precise = jnp.where(live > 0, joined[members + 1:members + 2, :], 0.0)
    scale = jnp.sqrt(precise * (1.0 / (members - 1)))
    obs = joined[0:members, :]
    mean = jnp.mean(obs, axis=0, keepdims=True)
    u[...] = (obs - mean) * scale
    return (joined[members:members + 1, :] - mean) * scale


def begin(members, own, live, u0, row0, inv0, p00, wrow):
    row0[...] = jnp.broadcast_to(scaled(own, live[...], members, u0), row0.shape)
    total = unit()
    for k in range(members // BLOCK):
        uk = u0[at(k), :]
        total = total + dot(left(uk, 0), right(uk, 0), 0, 0)
        p00[at(k), :] = total
    inverse_factors(p00, inv0, wrow)


def factor(members, u0, row0, inv0, before, after, live, *rest):
    store, u1, u2, l10, l20, l21, inv1, inv2, y0, y1, y2, s, p11, p21, p22, wrow, sems = rest
    kept = (u1, u2, l10, l20, l21, inv1, inv2, y0, y1, y2, s, u0, inv0)
    copies = [pltpu.make_async_copy(kept[i], store.at[pl.ds(i * members, members), :], sems.at[i]) for i in range(PARTS)]

    def send(*refs):
        for i in refs:
            copies[i].start()

    send(11, 12)
    eye = unit()
    first_row = lax.broadcasted_iota(jnp.int32, (BLOCK, BLOCK), 0) == 0
    row1 = scaled(before, live[0:1, :], members, u1)
    row2 = scaled(after, live[1:2, :], members, u2)
    send(0, 1)

    def forcing(ref, row, c):
        if c + 1 < CHAINS:
            return ref[at(c + 1), :]
        return jnp.where(first_row, row, 0.0)

    for c in range(CHAINS):
        got = dot(left(u1[at(c), :], 0), right(jnp.concatenate([u0[at(c), :], u1[at(c), :]], axis=1), 0), 0, 0)
        l10[at(c), :] = got[:, :BLOCK] + (l10[at(c - 1), :] if c else 0.0)
        p11[at(c), :] = got[:, BLOCK:] + (p11[at(c - 1), :] if c else eye)
    for c in range(CHAINS):
        l10[at(c), :] = dot(left(l10[at(c), :], 1), right(inv0[at(c), :], 1), 1, 1)
    send(2)
    for c in range(CHAINS):
        lhs, rhs = pair(l10[at(c), :])
        p11[at(c), :] -= dot(lhs, rhs, 1, 1)

    def gram(c):
        uk = [u0[at(c), :], u1[at(c), :], u2[at(c), :]]
        got = dot(left(uk[2], 0), right(jnp.concatenate(uk, axis=1), 0), 0, 0)
        l20[at(c), :] = got[:, :BLOCK] + (l20[at(c - 1), :] if c else 0.0)
        p21[at(c), :] = got[:, BLOCK:2 * BLOCK] + (p21[at(c - 1), :] if c else 0.0)
        p22[at(c), :] = got[:, 2 * BLOCK:] + (p22[at(c - 1), :] if c else eye)

    def low(c):
        rows = dot(left(jnp.concatenate([l20[at(c), :], forcing(u0, row0[0:1, :], c)], axis=0), 1),
                   right(inv0[at(c), :], 1), 1, 1)
        l20[at(c), :] = rows[:BLOCK]
        y0[at(c), :] = rows[BLOCK:]

    def take(c):
        lhs, rhs = pair(jnp.concatenate([l20[at(c), :], y0[at(c), :]], axis=0))
        upd = dot(lhs, jnp.concatenate([right(l10[at(c), :], 1), rhs[:BLOCK]], axis=0), 1, 1)
        p21[at(c), :] -= upd[:BLOCK, :BLOCK]
        p22[at(c), :] -= upd[:BLOCK, BLOCK:]
        y1[at(c), :] = forcing(u1, row1, c) - upd[BLOCK:, :BLOCK]
        y2[at(c), :] = forcing(u2, row2, c) - upd[BLOCK:, BLOCK:]
        if c + 1 < CHAINS:
            s[at(c + 1), :] = eye + dot(lhs[BLOCK:], rhs[BLOCK:], 1, 1)

    inverse_factors(p11, inv1, wrow, ((gram,), (low,), (take,)))
    send(3, 5, 7)
    for c in range(CHAINS):
        l21[at(c), :] = dot(left(p21[at(c), :], 1), right(inv1[at(c), :], 1), 1, 1)
    send(4)
    for c in range(CHAINS):
        lhs, rhs = pair(l21[at(c), :])
        p22[at(c), :] -= dot(lhs, rhs, 1, 1)

    def low_two(c):
        y1[at(c), :] = dot(left(y1[at(c), :], 1), right(inv1[at(c), :], 1), 1, 1)

    def take_two(c):
        lhs, rhs = pair(y1[at(c), :])
        upd = dot(lhs, jnp.concatenate([right(l21[at(c), :], 1), rhs], axis=0), 1, 1)
        y2[at(c), :] -= upd[:, :BLOCK]
        if c + 1 < CHAINS:
            s[at(c + 1), :] += upd[:, BLOCK:]
        else:
            lhs, rhs = pair(jnp.concatenate([u0[at(0), :], u1[at(0), :], u2[at(0), :]], axis=1))
            s[at(0), :] = eye + dot(lhs, rhs, 1, 1)

    inverse_factors(p22, inv2, wrow, ((low_two,), (take_two,)))
    send(6, 8)
    for c in range(CHAINS):
        y2[at(c), :] = dot(left(y2[at(c), :], 1), right(inv2[at(c), :], 1), 1, 1)
    send(9)
    for c in range(CHAINS - 1):
        lhs, rhs = pair(y2[at(c), :])
        s[at(c + 1), :] += dot(lhs, rhs, 1, 1)
    send(10)
    for copy in copies:
        copy.wait()


def apply(members, state, land, store, out, *rest):
    u1, u2, l10, l20, l21, inv1, inv2, y0, y1, y2, s, u0, inv0, f0, f1, f2, r, inv, wrow, sems = rest
    kept = (u1, u2, l10, l20, l21, inv1, inv2, y0, y1, y2, s, u0, inv0)
    copies = [pltpu.make_async_copy(store.at[pl.ds(i * members, members), :], kept[i], sems.at[i]) for i in range(PARTS)]
    for i in (10, 11, 0, 1, 12, 2, 3, 7, 5, 4, 8, 6, 9):
        copies[i].start()

    def need(c, *parts):
        for i in parts if c == 0 else ():
            copies[i].wait()

    state_mean = jnp.mean(state[...], axis=0, keepdims=True)
    need(0, 10)

    def gram(c):
        need(c, 11, 0, 1)
        uk = [u0[at(c), :], u1[at(c), :], u2[at(c), :]]
        got = dot(left(state[at(c), :] - state_mean, 0), right(jnp.concatenate(uk, axis=1), 0), 0, 0)
        for i, ref in enumerate((f0, f1, f2)):
            x = got[:, i * BLOCK:(i + 1) * BLOCK]
            ref[at(c + 1), :] = x + (ref[at(c), :] if c else 0.0)

    def low_one(c):
        need(c, 12)
        r[at(c), :] = dot(left(f0[at(c + 1), :], 1), right(inv0[at(c), :], 1), 1, 1)

    def take_one(c):
        need(c, 2, 3, 7)
        cols = jnp.concatenate([l10[at(c), :], l20[at(c), :], y0[at(c), :]], axis=0)
        upd = dot(left(r[at(c), :], 1), right(cols, 1), 1, 1)
        f1[at(c + 1), :] -= upd[:, :BLOCK]
        f2[at(c + 1), :] -= upd[:, BLOCK:2 * BLOCK]
        r[at(c), :] = upd[:, 2 * BLOCK:]

    def low_two(c):
        need(c, 5)
        f1[at(c + 1), :] = dot(left(f1[at(c + 1), :], 1), right(inv1[at(c), :], 1), 1, 1)

    def take_two(c):
        need(c, 4, 8)
        upd = dot(left(f1[at(c + 1), :], 1), right(jnp.concatenate([l21[at(c), :], y1[at(c), :]], axis=0), 1), 1, 1)
        f2[at(c + 1), :] -= upd[:, :BLOCK]
        r[at(c), :] += upd[:, BLOCK:]

    def low_three(c):
        need(c, 6)
        f2[at(c + 1), :] = dot(left(f2[at(c + 1), :], 1), right(inv2[at(c), :], 1), 1, 1)

    def take_three(c):
        need(c, 9)
        r[at(c), :] += dot(left(f2[at(c + 1), :], 1), right(y2[at(c), :], 1), 1, 1)

    inverse_factors(s, inv, wrow, ((gram,), (low_one, take_one), (low_two, take_two), (low_three, take_three)))
    increment = dot(left(unit()[:8], 1), right(r[at(CHAINS - 1), :], 1), 1, 1)[0:1, :]
    shift = state_mean + increment
    wet = land[0:1, :] > 0
    for k in range(members // BLOCK):
        back = state[at(k), :]
        t = left(inv[at(k), :], 1)
        spread = dot(t, right(back - state_mean, 0), 1, 0)
        if k > 0:
            spread = spread - dot(t, right(r[at(k - 1), :], 1), 1, 1)
        out[at(k), :] = jnp.where(wet, shift + spread, back)


PARTS = 13


def call(kernel, members, outs, scratch, flops, args, far_in=False, far_out=False):
    far, near = pl.BlockSpec(memory_space=pltpu.HBM), pl.BlockSpec(memory_space=pltpu.VMEM)
    return pl.pallas_call(
        lambda *refs: kernel(members, *refs),
        out_shape=tuple(jax.ShapeDtypeStruct((rows, BLOCK), jnp.float32) for rows in outs),
        in_specs=[near] * (len(args) - 1) + [far if far_in else near],
        out_specs=tuple([far if far_out else near] * len(outs)),
        scratch_shapes=[pltpu.VMEM((rows, BLOCK), jnp.float32) for rows in scratch]
        + [pltpu.VMEM((CHAINS * SUB, BLOCK), jnp.float32)] + [pltpu.SemaphoreType.DMA((PARTS,))] * (far_in or far_out),
        compiler_params=pltpu.CompilerParams(vmem_limit_bytes=40 * 1024 * 1024),
        cost_estimate=pl.CostEstimate(flops=flops, bytes_accessed=2_000_000, transcendentals=0),
    )(*args)


def start(own, live):
    n = own.shape[0] - 8
    return call(begin, n, (n, 8, n), (n,), 4_000_000_000, (own, live[0:1]))


def middle(u0, row0, inv0, before, after, live):
    n = u0.shape[0]
    return call(factor, n, (50 * n,), (n,) * 14, 10_000_000_000, (u0, row0, inv0, before, after, live[1:3]), far_out=True)[0]


def finish(state, land, mid):
    n = state.shape[0]
    return call(apply, n, (n,), (n,) * PARTS + (n + BLOCK,) * 3 + (n, n), 8_000_000_000, (state, land, mid), far_in=True)[0]


def compute(own, before, after, state, value, precise, land):
    info = jnp.stack([value, precise], axis=1)
    own, before, after = (jnp.concatenate([x, info[i], jnp.zeros((6, BLOCK), jnp.float32)]) for i, x in enumerate((own, before, after)))
    live = jnp.ones((3, BLOCK), jnp.int32)
    u0, row0, inv0 = start(own, live)
    return finish(state, land, middle(u0, row0, inv0, before, after, live))


def ring(x, step):
    count = lax.axis_size(("mem", "grp"))
    return lax.ppermute(x, ("mem", "grp"), [(i, (i + step) % count) for i in range(count)])


def local(state, obs_ens, obs_value, obs_precision, locality, obs_count, land_mask):
    spots = jnp.arange(3 * BLOCK, dtype=jnp.int32).reshape(3, BLOCK)
    spots = jnp.stack([spots[1], spots[0], spots[2]], axis=0)
    rank = jnp.arange(locality.shape[1], dtype=jnp.int32)
    live = jnp.where(rank < obs_count[0], locality[0], -1)
    live = jnp.any(spots[:, None, :] == live[None, :, None], axis=1).astype(jnp.int32)
    whole_obs = lax.all_to_all(obs_ens, "grp", split_axis=1, concat_axis=0, tiled=True)[:, 0, :]
    whole_obs, turned = lax.optimization_barrier((whole_obs, jnp.swapaxes(state, 0, 1)))
    own = jnp.concatenate([whole_obs, obs_value, obs_precision, jnp.zeros((6, BLOCK), jnp.float32)], axis=0)
    before, after = ring(own, 1), ring(own, -1)
    u0, row0, inv0 = start(own, live)
    turned, inv0 = lax.optimization_barrier((turned, inv0))
    whole_state = lax.all_to_all(turned, "grp", split_axis=0, concat_axis=0, tiled=True).reshape(-1, BLOCK)
    mid = middle(u0, row0, inv0, before, after, live)
    out = finish(whole_state, land_mask, mid)
    return out[:, None, :]


def solution(mesh):
    placed = (
        P("grp", "mem", None),
        P("grp", "mem", None),
        P(("mem", "grp"), None),
        P(("mem", "grp"), None),
        P(("mem", "grp"), None),
        P(("mem", "grp")),
        P(("mem", "grp"), None),
    )
    return jax.shard_map(
        local, mesh=mesh, in_specs=placed, out_specs=P(None, ("mem", "grp"), None), check_vma=False
    )
```

```python
import jax
import jax.numpy as jnp
from jax import lax
from jax.experimental import pallas as pl
from jax.experimental.pallas import tpu as pltpu
from jax.sharding import PartitionSpec as P

CHAINS = 8
SUB = 16
CUT = 4
BLOCK = 128


def lane(x, i):
    return jnp.broadcast_to(x[:, i:i + 1], x.shape)


def split(x):
    hi = x.astype(jnp.bfloat16)
    rest = x - hi.astype(jnp.float32)
    mid = rest.astype(jnp.bfloat16)
    lo = (rest - mid.astype(jnp.float32)).astype(jnp.bfloat16)
    return hi, mid, lo


def left(x, axis):
    hi, mid, lo = split(x)
    return jnp.concatenate([hi, hi, mid, hi, lo, mid], axis=axis)


def right(x, axis):
    hi, mid, lo = split(x)
    return jnp.concatenate([hi, mid, hi, lo, hi, mid], axis=axis)


def pair(x):
    hi, mid, lo = split(x)
    return (jnp.concatenate([hi, hi, mid, hi, lo, mid], axis=1), jnp.concatenate([hi, mid, hi, lo, hi, mid], axis=1))


def dot(a, b, ca, cb):
    return lax.dot_general(a, b, (((ca,), (cb,)), ((), ())), preferred_element_type=jnp.float32)


def sub_block(mat, inv, wrow, q):
    iota = lax.broadcasted_iota(jnp.int32, (CHAINS, BLOCK), 1)
    base = q * SUB
    panels = SUB // 8

    def block(rows, first):
        return {(a, b): lane(rows[a], first + b) for a in range(8) for b in range(a, 8)}

    groups = [
        [mat[pl.ds(base + 8 * r + a, CHAINS, stride=BLOCK), :] for a in range(8)]
        for r in range(panels)
    ]
    coef = block(groups[0], base)
    for p in range(panels):
        first = base + 8 * p
        inside = (iota >= first) & (iota < first + 8)
        rows = [jnp.where(inside, jnp.where(iota == first + a, 1.0, 0.0), groups[p][a]) for a in range(8)]
        for r in range(p + 1, panels):
            groups[r] = [jnp.where(inside, 0.0, x) for x in groups[r]]
        done = []
        ahead = None
        for t in range(8):
            scale = lax.rsqrt(coef[t, t])
            w = rows[t] * scale
            done.append(w)
            inv[pl.ds(first + t, CHAINS, stride=BLOCK), :] = jnp.where(iota <= first + t, w, 0.0)
            wrow[pl.ds(8 * p + t, CHAINS, stride=SUB), :] = w
            m = {a: coef[t, a] * scale for a in range(t + 1, 8)}
            for a in range(t + 1, 8):
                for b in range(a, 8):
                    coef[a, b] = coef[a, b] - m[a] * m[b]
                rows[a] = rows[a] - m[a] * w
            if p + 1 < panels:
                if t == CUT:
                    ahead = block(groups[p + 1], first + 8)
                c = [lane(w, first + 8 + a) for a in range(8)]
                for a in range(8):
                    groups[p + 1][a] = groups[p + 1][a] - c[a] * w
                if t >= CUT:
                    for a in range(8):
                        for b in range(a, 8):
                            ahead[a, b] = ahead[a, b] - c[a] * c[b]
        if p + 1 < panels:
            coef = ahead
            for r in range(p + 2, panels):
                for a in range(8):
                    x = groups[r][a]
                    for t in range(8):
                        x = x - lane(done[t], base + 8 * r + a) * done[t]
                    groups[r][a] = x


def join(mat, wrow, q):
    base = q * SUB
    lanes = lax.broadcasted_iota(jnp.int32, (SUB, BLOCK), 1)
    drop = (lanes > lax.broadcasted_iota(jnp.int32, (SUB, BLOCK), 0) + base) & (lanes < base + SUB)
    below = BLOCK - base - SUB
    over = lax.broadcasted_iota(jnp.int32, (below, BLOCK), 1)
    clear = (over >= base) & (over < base + SUB)
    for c in range(CHAINS):
        w = wrow[c * SUB:(c + 1) * SUB, :]
        out = dot(left(w, 0), right(jnp.where(drop, 0.0, w), 0), 0, 0)
        at = pl.ds(c * BLOCK + base + SUB, below)
        mat[at, :] = jnp.where(clear, 0.0, mat[at, :]) - out[base + SUB:, :]


def inverse_factors(mat, inv, wrow, stages=()):
    def beside(q):
        for step in range(max((len(group) for group in stages), default=0)):
            for d, group in enumerate(stages):
                if step < len(group) and 0 <= q - d < CHAINS:
                    group[step](q - d)

    count = BLOCK // SUB
    for q in range(count):
        sub_block(mat, inv, wrow, q)
        beside(q)
        if q + 1 < count:
            join(mat, wrow, q)
    for q in range(count, count + len(stages) - 1):
        beside(q)


def at(k):
    return pl.ds(k * BLOCK, BLOCK)


def unit():
    return (lax.broadcasted_iota(jnp.int32, (BLOCK, BLOCK), 0)
            == lax.broadcasted_iota(jnp.int32, (BLOCK, BLOCK), 1)).astype(jnp.float32)


def scaled(joined, live, members, u):
    precise = jnp.where(live > 0, joined[members + 1:members + 2, :], 0.0)
    scale = jnp.sqrt(precise * (1.0 / (members - 1)))
    obs = joined[0:members, :]
    mean = jnp.mean(obs, axis=0, keepdims=True)
    u[...] = (obs - mean) * scale
    return (joined[members:members + 1, :] - mean) * scale


def begin(members, own, live, u0, row0, inv0, p00, wrow):
    row0[...] = jnp.broadcast_to(scaled(own, live[...], members, u0), row0.shape)
    total = unit()
    for k in range(members // BLOCK):
        uk = u0[at(k), :]
        total = total + dot(left(uk, 0), right(uk, 0), 0, 0)
        p00[at(k), :] = total
    inverse_factors(p00, inv0, wrow)


def factor(members, u0, row0, inv0, before, after, live, *rest):
    store, u1, u2, l10, l20, l21, inv1, inv2, y0, y1, y2, s, p11, p21, p22, wrow, sems = rest
    kept = (u1, u2, l10, l20, l21, inv1, inv2, y0, y1, y2, s, u0, inv0)
    copies = [pltpu.make_async_copy(kept[i], store.at[pl.ds(i * members, members), :], sems.at[i]) for i in range(PARTS)]

    def send(*refs):
        for i in refs:
            copies[i].start()

    send(11, 12)
    eye = unit()
    first_row = lax.broadcasted_iota(jnp.int32, (BLOCK, BLOCK), 0) == 0
    row1 = scaled(before, live[0:1, :], members, u1)
    row2 = scaled(after, live[1:2, :], members, u2)
    send(0, 1)

    def forcing(ref, row, c):
        if c + 1 < CHAINS:
            return ref[at(c + 1), :]
        return jnp.where(first_row, row, 0.0)

    for c in range(CHAINS):
        got = dot(left(u1[at(c), :], 0), right(jnp.concatenate([u0[at(c), :], u1[at(c), :]], axis=1), 0), 0, 0)
        l10[at(c), :] = got[:, :BLOCK] + (l10[at(c - 1), :] if c else 0.0)
        p11[at(c), :] = got[:, BLOCK:] + (p11[at(c - 1), :] if c else eye)
    for c in range(CHAINS):
        l10[at(c), :] = dot(left(l10[at(c), :], 1), right(inv0[at(c), :], 1), 1, 1)
    send(2)
    for c in range(CHAINS):
        lhs, rhs = pair(l10[at(c), :])
        p11[at(c), :] -= dot(lhs, rhs, 1, 1)

    def gram(c):
        uk = [u0[at(c), :], u1[at(c), :], u2[at(c), :]]
        got = dot(left(uk[2], 0), right(jnp.concatenate(uk, axis=1), 0), 0, 0)
        l20[at(c), :] = got[:, :BLOCK] + (l20[at(c - 1), :] if c else 0.0)
        p21[at(c), :] = got[:, BLOCK:2 * BLOCK] + (p21[at(c - 1), :] if c else 0.0)
        p22[at(c), :] = got[:, 2 * BLOCK:] + (p22[at(c - 1), :] if c else eye)

    def low(c):
        rows = dot(left(jnp.concatenate([l20[at(c), :], forcing(u0, row0[0:1, :], c)], axis=0), 1),
                   right(inv0[at(c), :], 1), 1, 1)
        l20[at(c), :] = rows[:BLOCK]
        y0[at(c), :] = rows[BLOCK:]

    def take(c):
        lhs, rhs = pair(jnp.concatenate([l20[at(c), :], y0[at(c), :]], axis=0))
        upd = dot(lhs, jnp.concatenate([right(l10[at(c), :], 1), rhs[:BLOCK]], axis=0), 1, 1)
        p21[at(c), :] -= upd[:BLOCK, :BLOCK]
        p22[at(c), :] -= upd[:BLOCK, BLOCK:]
        y1[at(c), :] = forcing(u1, row1, c) - upd[BLOCK:, :BLOCK]
        y2[at(c), :] = forcing(u2, row2, c) - upd[BLOCK:, BLOCK:]
        if c + 1 < CHAINS:
            s[at(c + 1), :] = eye + dot(lhs[BLOCK:], rhs[BLOCK:], 1, 1)

    inverse_factors(p11, inv1, wrow, ((gram,), (low,), (take,)))
    send(3, 5, 7)
    for c in range(CHAINS):
        l21[at(c), :] = dot(left(p21[at(c), :], 1), right(inv1[at(c), :], 1), 1, 1)
    send(4)
    for c in range(CHAINS):
        lhs, rhs = pair(l21[at(c), :])
        p22[at(c), :] -= dot(lhs, rhs, 1, 1)

    def low_two(c):
        y1[at(c), :] = dot(left(y1[at(c), :], 1), right(inv1[at(c), :], 1), 1, 1)

    def take_two(c):
        lhs, rhs = pair(y1[at(c), :])
        upd = dot(lhs, jnp.concatenate([right(l21[at(c), :], 1), rhs], axis=0), 1, 1)
        y2[at(c), :] -= upd[:, :BLOCK]
        if c + 1 < CHAINS:
            s[at(c + 1), :] += upd[:, BLOCK:]
        else:
            lhs, rhs = pair(jnp.concatenate([u0[at(0), :], u1[at(0), :], u2[at(0), :]], axis=1))
            s[at(0), :] = eye + dot(lhs, rhs, 1, 1)

    inverse_factors(p22, inv2, wrow, ((low_two,), (take_two,)))
    send(6, 8)
    for c in range(CHAINS):
        y2[at(c), :] = dot(left(y2[at(c), :], 1), right(inv2[at(c), :], 1), 1, 1)
    send(9)
    for c in range(CHAINS - 1):
        lhs, rhs = pair(y2[at(c), :])
        s[at(c + 1), :] += dot(lhs, rhs, 1, 1)
    send(10)
    for copy in copies:
        copy.wait()


def apply(members, state, land, store, out, *rest):
    u1, u2, l10, l20, l21, inv1, inv2, y0, y1, y2, s, u0, inv0, f0, f1, f2, r, inv, wrow, sems = rest
    kept = (u1, u2, l10, l20, l21, inv1, inv2, y0, y1, y2, s, u0, inv0)
    copies = [pltpu.make_async_copy(store.at[pl.ds(i * members, members), :], kept[i], sems.at[i]) for i in range(PARTS)]
    for i in (10, 11, 0, 1):
        copies[i].start()

    def need(c, *parts):
        for i in parts if c == 0 else ():
            copies[i].wait()

    state_mean = jnp.mean(state[...], axis=0, keepdims=True)
    need(0, 10)
    for i in (12, 2, 3, 7, 5, 4, 8, 6, 9):
        copies[i].start()

    def gram(c):
        need(c, 11, 0, 1)
        uk = [u0[at(c), :], u1[at(c), :], u2[at(c), :]]
        got = dot(left(state[at(c), :] - state_mean, 0), right(jnp.concatenate(uk, axis=1), 0), 0, 0)
        for i, ref in enumerate((f0, f1, f2)):
            x = got[:, i * BLOCK:(i + 1) * BLOCK]
            ref[at(c + 1), :] = x + (ref[at(c), :] if c else 0.0)

    def low_one(c):
        need(c, 12)
        r[at(c), :] = dot(left(f0[at(c + 1), :], 1), right(inv0[at(c), :], 1), 1, 1)

    def take_one(c):
        need(c, 2, 3, 7)
        cols = jnp.concatenate([l10[at(c), :], l20[at(c), :], y0[at(c), :]], axis=0)
        upd = dot(left(r[at(c), :], 1), right(cols, 1), 1, 1)
        f1[at(c + 1), :] -= upd[:, :BLOCK]
        f2[at(c + 1), :] -= upd[:, BLOCK:2 * BLOCK]
        r[at(c), :] = upd[:, 2 * BLOCK:]

    def low_two(c):
        need(c, 5)
        f1[at(c + 1), :] = dot(left(f1[at(c + 1), :], 1), right(inv1[at(c), :], 1), 1, 1)

    def take_two(c):
        need(c, 4, 8)
        upd = dot(left(f1[at(c + 1), :], 1), right(jnp.concatenate([l21[at(c), :], y1[at(c), :]], axis=0), 1), 1, 1)
        f2[at(c + 1), :] -= upd[:, :BLOCK]
        r[at(c), :] += upd[:, BLOCK:]

    def low_three(c):
        need(c, 6)
        f2[at(c + 1), :] = dot(left(f2[at(c + 1), :], 1), right(inv2[at(c), :], 1), 1, 1)

    def take_three(c):
        need(c, 9)
        r[at(c), :] += dot(left(f2[at(c + 1), :], 1), right(y2[at(c), :], 1), 1, 1)

    inverse_factors(s, inv, wrow, ((gram,), (low_one, take_one), (low_two, take_two), (low_three, take_three)))
    increment = dot(left(unit()[:8], 1), right(r[at(CHAINS - 1), :], 1), 1, 1)[0:1, :]
    shift = state_mean + increment
    wet = land[0:1, :] > 0
    for k in range(members // BLOCK):
        back = state[at(k), :]
        t = left(inv[at(k), :], 1)
        spread = dot(t, right(back - state_mean, 0), 1, 0)
        if k > 0:
            spread = spread - dot(t, right(r[at(k - 1), :], 1), 1, 1)
        out[at(k), :] = jnp.where(wet, shift + spread, back)


PARTS = 13


def call(kernel, members, outs, scratch, flops, args, far_in=False, far_out=False):
    far, near = pl.BlockSpec(memory_space=pltpu.HBM), pl.BlockSpec(memory_space=pltpu.VMEM)
    return pl.pallas_call(
        lambda *refs: kernel(members, *refs),
        out_shape=tuple(jax.ShapeDtypeStruct((rows, BLOCK), jnp.float32) for rows in outs),
        in_specs=[near] * (len(args) - 1) + [far if far_in else near],
        out_specs=tuple([far if far_out else near] * len(outs)),
        scratch_shapes=[pltpu.VMEM((rows, BLOCK), jnp.float32) for rows in scratch]
        + [pltpu.VMEM((CHAINS * SUB, BLOCK), jnp.float32)] + [pltpu.SemaphoreType.DMA((PARTS,))] * (far_in or far_out),
        compiler_params=pltpu.CompilerParams(vmem_limit_bytes=40 * 1024 * 1024),
        cost_estimate=pl.CostEstimate(flops=flops, bytes_accessed=2_000_000, transcendentals=0),
    )(*args)


def start(own, live):
    n = own.shape[0] - 8
    return call(begin, n, (n, 8, n), (n,), 4_000_000_000, (own, live[0:1]))


def middle(u0, row0, inv0, before, after, live):
    n = u0.shape[0]
    return call(factor, n, (50 * n,), (n,) * 14, 10_000_000_000, (u0, row0, inv0, before, after, live[1:3]), far_out=True)[0]


def finish(state, land, mid):
    n = state.shape[0]
    return call(apply, n, (n,), (n,) * PARTS + (n + BLOCK,) * 3 + (n, n), 8_000_000_000, (state, land, mid), far_in=True)[0]


def compute(own, before, after, state, value, precise, land):
    info = jnp.stack([value, precise], axis=1)
    own, before, after = (jnp.concatenate([x, info[i], jnp.zeros((6, BLOCK), jnp.float32)]) for i, x in enumerate((own, before, after)))
    live = jnp.ones((3, BLOCK), jnp.int32)
    u0, row0, inv0 = start(own, live)
    return finish(state, land, middle(u0, row0, inv0, before, after, live))


def ring(x, step):
    count = lax.axis_size(("mem", "grp"))
    return lax.ppermute(x, ("mem", "grp"), [(i, (i + step) % count) for i in range(count)])


def local(state, obs_ens, obs_value, obs_precision, locality, obs_count, land_mask):
    spots = jnp.arange(3 * BLOCK, dtype=jnp.int32).reshape(3, BLOCK)
    spots = jnp.stack([spots[1], spots[0], spots[2]], axis=0)
    rank = jnp.arange(locality.shape[1], dtype=jnp.int32)
    live = jnp.where(rank < obs_count[0], locality[0], -1)
    live = jnp.any(spots[:, None, :] == live[None, :, None], axis=1).astype(jnp.int32)
    whole_obs = lax.all_to_all(obs_ens, "grp", split_axis=1, concat_axis=0, tiled=True)[:, 0, :]
    whole_obs, turned = lax.optimization_barrier((whole_obs, jnp.swapaxes(state, 0, 1)))
    own = jnp.concatenate([whole_obs, obs_value, obs_precision, jnp.zeros((6, BLOCK), jnp.float32)], axis=0)
    before, after = ring(own, 1), ring(own, -1)
    u0, row0, inv0 = start(own, live)
    turned, inv0 = lax.optimization_barrier((turned, inv0))
    whole_state = lax.all_to_all(turned, "grp", split_axis=0, concat_axis=0, tiled=True).reshape(-1, BLOCK)
    mid = middle(u0, row0, inv0, before, after, live)
    out = finish(whole_state, land_mask, mid)
    return out[:, None, :]


def solution(mesh):
    placed = (
        P("grp", "mem", None),
        P("grp", "mem", None),
        P(("mem", "grp"), None),
        P(("mem", "grp"), None),
        P(("mem", "grp"), None),
        P(("mem", "grp")),
        P(("mem", "grp"), None),
    )
    return jax.shard_map(
        local, mesh=mesh, in_specs=placed, out_specs=P(None, ("mem", "grp"), None), check_vma=False
    )
```
